128 devices in a mesh: pipe: 2 (over y_hi), section: 8 (over x, y_lo), tp: 8 (over z, core).
Axes of the slice: x: 4, y: 4 (y_hi: 2, y_lo: 2; y = y_hi * 2 + y_lo), z: 4, core: 2. Of those that a mesh axis runs over, the one named last changes fastest.
Arguments:
- acts: bfloat16 [2, 16, 1536, 8192], P('pipe', 'section', None, 'tp'), may hold values from -6 to 6
- kv_grads: bfloat16 [2, 16, 1536, 2048], P('pipe', 'section', None, 'tp'), may hold values from -0.15625 to 0.15625
- layer_section: int32 [2, 12], replicated, may hold values from 0 to 7, as said below
- token_counts: int32 [2], replicated, may hold values from 768 to 1536, as said below
Outputs:
- summed_grads: bfloat16 [16, 8192, 2048], P('section', 'tp', 'pipe')
The draws below stay inside these ranges and needn't reach their ends.
Inputs may be any that keep to these rules, and one draw needn't show every extreme that they name: `layer_section`: in each relay the section never falls as the layer index rises, every section holds 1 or 2 layers, sections 2 k and 2 k + 1 hold 3 layers together, and a layer's sections in the two relays differ by at most 1, by exactly 1 for some layer. `token_counts`: for one of the two relays it equals 1536.
All inputs are finite; a program needn't handle non-finite values.
Results may differ from the reference program's by a relative error of at most 0.0052.
Values may be sent and summed in bfloat16 or wider, within the bound.
No kernel may reach another device: no remote copies, remote signals or barrier semaphores. Data moves between devices by JAX's collectives and lax.ppermute only.
A program may use at most 128 MiB of HBM per device.

```python
import jax
import jax.numpy as jnp
from jax import lax

D = 8192
N_KV = 8
HD = 128
TOK = 1536
SLOTS = 2
LAYERS = 12
N_SECTION = 8


def draw_layer_section(key, part):
    key = jax.random.fold_in(key, 11)
    pair_total = N_SECTION // 2
    orients = jax.random.randint(key, (2, pair_total), 0, 2)
    orients = orients.at[1, 0].set(1 - orients[0, 0])
    layer_ids = jnp.arange(LAYERS, dtype=jnp.int32)
    pair_ids = layer_ids // 3
    within = layer_ids % 3
    chosen = orients[:, pair_ids]
    later = jnp.where(chosen == 0, (within == 2)[None, :], (within >= 1)[None, :]).astype(jnp.int32)
    return (2 * pair_ids[None, :] + later).astype(jnp.int32)


def draw_token_counts(key, part):
    key = jax.random.fold_in(key, 12)
    first_key, second_key = jax.random.split(key)
    counts = jax.random.randint(first_key, (2,), TOK // 2, TOK + 1)
    full_pipe = jax.random.randint(second_key, (), 0, 2)
    counts = jnp.where(jnp.arange(2) == full_pipe, TOK, counts)
    return counts.astype(jnp.int32)


def steps_of(key, extent, cuts, least, high):
    level, own = 1.0, jax.random.fold_in(key, 6)
    for axis_at, shards_of in cuts:
        draws = jnp.exp(jax.random.uniform(jax.random.fold_in(own, axis_at), (shards_of,), jnp.float32, least / len(cuts), high / len(cuts)))
        level = level * jnp.repeat(draws, extent[axis_at] // shards_of).reshape([-1 if axis == axis_at else 1 for axis in range(len(extent))])
    return level


def normal_values(key, shape, spread, limit, shards=(), held_as=jnp.bfloat16):
    array = jax.random.normal(key, shape, jnp.float32) * spread
    if len(shards) > 0:
        array = steps_of(key, shape, shards, -0.22, 0.18) * array
    return jnp.clip(array, min=-limit, max=limit).astype(held_as)


def setup_inputs(seed: int = 0) -> dict:
    splits = jax.random.split(jax.random.key(seed), 5)
    acts = normal_values(splits[0], (2, N_SECTION * SLOTS, TOK, D), 1.0, 6.0, ((0, 2), (1, 8), (3, 8)))
    kv_grads = normal_values(splits[1], (2, N_SECTION * SLOTS, TOK, 2 * N_KV * HD), TOK ** -0.5, 0.15625, ((0, 2), (1, 8), (3, 8)))
    layer_section = draw_layer_section(jax.random.fold_in(splits[4], 71), 0)
    token_counts = draw_token_counts(jax.random.fold_in(splits[4], 71), 0)
    return {"acts": acts, "kv_grads": kv_grads, "layer_section": layer_section, "token_counts": token_counts}


def slot_table(section_row, section_total, slot_count):
    section_ids = jnp.arange(section_total, dtype=jnp.int32)
    first_layer = jnp.sum((section_row[None, :] < section_ids[:, None]).astype(jnp.int32), axis=1).astype(jnp.int32)
    layer_count = jnp.sum((section_row[None, :] == section_ids[:, None]).astype(jnp.int32), axis=1).astype(jnp.int32)
    offsets = jnp.arange(slot_count, dtype=jnp.int32)
    slot_layers = jnp.where(offsets[None, :] < layer_count[:, None], first_layer[:, None] + offsets[None, :], -1)
    return slot_layers.reshape(-1).astype(jnp.int32)


def reference(acts, kv_grads, layer_section, token_counts):
    slot_total = N_SECTION * SLOTS
    half_width = N_KV * HD
    positions = jnp.arange(slot_total, dtype=jnp.int32)
    row_ids = jnp.arange(TOK, dtype=jnp.int32)
    layouts = [slot_table(layer_section[0], N_SECTION, SLOTS), slot_table(layer_section[1], N_SECTION, SLOTS)]

    def gradient(pipe_index, layer_id, column_half):
        slot_index = jnp.sum(jnp.where(layouts[pipe_index] == layer_id, positions, 0)).astype(jnp.int32)
        inputs = lax.dynamic_index_in_dim(acts[pipe_index], slot_index, 0, keepdims=False)
        kv_rows = lax.dynamic_index_in_dim(kv_grads[pipe_index], slot_index, 0, keepdims=False)
        kv_rows = kv_rows[:, column_half * half_width:(column_half + 1) * half_width]
        live_rows = (row_ids < token_counts[pipe_index])[:, None]
        kv_rows = jnp.where(live_rows, kv_rows, jnp.zeros_like(kv_rows))
        return jnp.dot(inputs.T, kv_rows, preferred_element_type=jnp.float32).astype(jnp.bfloat16)

    def one_slot(position):
        blocks = []
        for column_half in (0, 1):
            layer_id = layouts[column_half][position]
            safe_layer = jnp.maximum(layer_id, 0).astype(jnp.int32)
            summed = gradient(0, safe_layer, column_half).astype(jnp.float32) + gradient(1, safe_layer, column_half).astype(jnp.float32)
            blocks.append(jnp.where(layer_id >= 0, summed, jnp.zeros_like(summed)).astype(jnp.bfloat16))
        return jnp.concatenate(blocks, axis=1)

    return lax.map(one_slot, positions)
```

```python
import functools

import jax
import jax.numpy as jnp
from jax import lax
from jax.experimental import pallas as pl
from jax.experimental.pallas import tpu as pltpu
from jax.sharding import PartitionSpec as P

MIB = 1 << 20
SETS = 2


def tied(*values):
    return lax.optimization_barrier(values)


def turn_kernel(pick, x_ref, o_ref):
    tile = x_ref.shape[1]
    rows = pl.program_id(1) * tile + lax.broadcasted_iota(jnp.int32, (tile, 1), 0)
    x = jnp.where(rows < pick[2], x_ref[0].astype(jnp.float32), 0.0)
    o_ref[0] = x.T.astype(o_ref.dtype)


def turn(pick, acts):
    slots, tokens, feats = acts.shape
    tile = 256
    return pl.pallas_call(
        turn_kernel,
        grid_spec=pltpu.PrefetchScalarGridSpec(
            num_scalar_prefetch=1,
            grid=(slots, tokens // tile),
            in_specs=[pl.BlockSpec((1, tile, feats), lambda s, i, p: (p[s], i, 0))],
            out_specs=pl.BlockSpec((1, feats, tile), lambda s, i, p: (s, 0, i)),
        ),
        out_shape=jax.ShapeDtypeStruct((slots, feats, tokens), acts.dtype),
        compiler_params=pltpu.CompilerParams(vmem_limit_bytes=24 * MIB),
        cost_estimate=pl.CostEstimate(flops=0, bytes_accessed=4 * acts.size, transcendentals=0),
    )(pick, acts)


def product(x_ref, kv_ref):
    kv = jnp.concatenate([kv_ref[t, 0] for t in range(kv_ref.shape[0])], axis=1)
    return jnp.dot(x_ref[0], kv, preferred_element_type=jnp.float32)


def send_kernel(pick, x_ref, kv_ref, o_ref):
    o_ref[...] = product(x_ref, kv_ref).astype(o_ref.dtype)


def send_block(pick, turned, kv):
    _, feats, tokens = turned.shape
    sources, _, _, width = kv.shape
    tile = 256
    out = (feats // 2, sources // 2 * width)
    return pl.pallas_call(
        send_kernel,
        grid_spec=pltpu.PrefetchScalarGridSpec(
            num_scalar_prefetch=1,
            grid=(out[0] // tile,),
            in_specs=[
                pl.BlockSpec((1, tile, tokens), lambda i, p: (p[0], p[1] * (out[0] // tile) + i, 0)),
                pl.BlockSpec((sources // 2, 1, tokens, width), lambda i, p: (p[3], p[2], 0, 0)),
            ],
            out_specs=pl.BlockSpec((tile, out[1]), lambda i, p: (i, 0)),
        ),
        out_shape=jax.ShapeDtypeStruct(out, turned.dtype),
        compiler_params=pltpu.CompilerParams(vmem_limit_bytes=24 * MIB),
        cost_estimate=pl.CostEstimate(
            flops=2 * out[0] * out[1] * tokens,
            bytes_accessed=2 * (out[0] * tokens + tokens * out[1] + out[0] * out[1]),
            transcendentals=0,
        ),
    )(pick, turned, kv)


def own_kernel(pick, x_ref, kv_ref, o_ref):
    o_ref[0] = product(x_ref, kv_ref).astype(o_ref.dtype)


def own_block(pick, turned, kv):
    slots, feats, tokens = turned.shape
    sources, _, _, width = kv.shape
    tile = 256
    cols = sources // 2 * width
    return pl.pallas_call(
        own_kernel,
        grid_spec=pltpu.PrefetchScalarGridSpec(
            num_scalar_prefetch=1,
            grid=(slots, feats // tile),
            in_specs=[
                pl.BlockSpec((1, tile, tokens), lambda s, i, p: (s, i, 0)),
                pl.BlockSpec((sources // 2, 1, tokens, width), lambda s, i, p: (p[2], p[s], 0, 0)),
            ],
            out_specs=pl.BlockSpec((1, tile, cols), lambda s, i, p: (s, i, 0)),
        ),
        out_shape=jax.ShapeDtypeStruct((slots, feats, cols), turned.dtype),
        compiler_params=pltpu.CompilerParams(vmem_limit_bytes=24 * MIB),
        cost_estimate=pl.CostEstimate(
            flops=2 * slots * feats * cols * tokens,
            bytes_accessed=2 * slots * (feats * tokens + tokens * cols + feats * cols),
            transcendentals=0,
        ),
    )(pick, turned, kv)


def join_kernel(width, pick, *refs):
    own, arrived, o_ref = refs[:SETS], refs[SETS:-1], refs[-1]
    code = pick[2 + pl.program_id(0) * 2 + pl.program_id(1)]
    count = len(arrived) // SETS
    span = SETS * width

    @pl.when(code == count)
    def _():
        o_ref[...] = jnp.zeros_like(o_ref)

    for choice in range(count):

        @pl.when(code == choice)
        def _():
            for c in range(SETS):
                total = own[c][0].astype(jnp.float32) + arrived[c * count + choice][...].astype(jnp.float32)
                total = total.astype(o_ref.dtype)
                for t in range(total.shape[1] // width):
                    o_ref[0, :, t * span + c * width : t * span + (c + 1) * width] = total[:, t * width : (t + 1) * width]


def join(pick, own, arrived, width):
    slots, feats, cols = own[0].shape
    half = feats // 2
    flat = [block for blocks in arrived for block in blocks]
    return pl.pallas_call(
        functools.partial(join_kernel, width),
        grid_spec=pltpu.PrefetchScalarGridSpec(
            num_scalar_prefetch=1,
            grid=(slots, 2),
            in_specs=[pl.BlockSpec((1, half, cols), lambda s, h, p: (p[s], h, 0))] * SETS
            + [pl.BlockSpec((half, cols), lambda s, h, p: (0, 0))] * len(flat),
            out_specs=pl.BlockSpec((1, half, SETS * cols), lambda s, h, p: (s, h, 0)),
        ),
        out_shape=jax.ShapeDtypeStruct((slots, feats, SETS * cols), own[0].dtype),
        compiler_params=pltpu.CompilerParams(vmem_limit_bytes=32 * MIB),
        cost_estimate=pl.CostEstimate(flops=0, bytes_accessed=14 * MIB, transcendentals=0),
    )(pick, *own, *flat)


def shards(acts, kv_grads, layer_section, token_counts):
    sections = lax.axis_size("section")
    pipe = lax.axis_index("pipe")
    section = lax.axis_index("section")
    acts, kv = acts[0], kv_grads[0]
    width = kv.shape[2] // SETS
    counts = jnp.sum((layer_section == section).astype(jnp.int32), axis=1)
    own_count = lax.dynamic_index_in_dim(counts, pipe, 0, keepdims=False)
    other_count = lax.dynamic_index_in_dim(counts, 1 - pipe, 0, keepdims=False)
    heavy = own_count == 2
    matched = own_count == other_count
    limit = lax.dynamic_index_in_dim(token_counts, pipe, 0, keepdims=False)
    h = heavy.astype(jnp.int32)
    f_slot = jnp.where(heavy, section % 2, 0)
    m_slot = 1 - f_slot

    def across(array):
        pairs = [
            (p * sections + s, (1 - p) * sections + (s ^ 1)) for p in range(2) for s in range(sections)
        ]
        return lax.ppermute(array, ("pipe", "section"), pairs)

    def beside(array):
        return lax.ppermute(array, "section", [(s, s ^ 1) for s in range(sections)])

    def scalars(*values):
        return jnp.stack([jnp.asarray(v, jnp.int32) for v in values])

    slot_of = lambda role: jnp.where(role == 1, m_slot, f_slot)
    other = 1 - pipe
    picks = [
        scalars(h, 0, slot_of(h), other),
        scalars(0, 1 - h, f_slot, other),
        scalars(1, 1, m_slot, other),
        scalars(0, 1, f_slot, other),
    ]
    gathered = []
    for c in range(SETS):
        part = kv[:, :, c * width : (c + 1) * width]
        if gathered:
            part, gathered[-1] = tied(part, gathered[-1])
        gathered.append(lax.all_gather(part, "tp", axis=0, tiled=False))
    turned = turn(scalars(f_slot, m_slot, limit), acts)
    own, arrived = [], []
    for c in range(SETS):
        kvs = gathered[c]
        sends = []
        for pick in picks:
            sends.append(send_block(pick, turned, kvs))
            turned, sends[-1] = tied(turned, sends[-1])
        c1, i1, x2, s2 = sends
        rc1, ri1, x2, s2 = tied(across(c1), beside(i1), x2, s2)
        c2, i2 = jnp.where(heavy, x2, ri1), jnp.where(heavy, s2, rc1)
        c2, i2, turned = tied(c2, i2, turned)
        rc2, ri2 = across(c2), beside(i2)
        own.append(own_block(scalars(f_slot, m_slot, pipe), turned, kvs))
        rc2, ri2, own[-1] = tied(rc2, ri2, own[-1])
        c3, i3 = jnp.where(heavy, ri1, ri2), jnp.where(heavy, rc1, rc2)
        if c + 1 < SETS:
            c3, i3, gathered[c + 1] = tied(c3, i3, gathered[c + 1])
        rc3, ri3 = across(c3), beside(i3)
        arrived.append((rc1, rc2, rc3, ri2, ri3))
    at_c1, at_c2, at_c3, at_i2, at_i3, none = range(6)
    fa = jnp.where(heavy == matched, at_c2, jnp.where(heavy, at_i2, at_i3))
    ma = jnp.where(heavy, jnp.where(matched, at_i2, at_c1), none)
    mb = jnp.where(heavy, jnp.where(matched, at_i3, at_c2), none)
    f_first = f_slot == 0
    codes = scalars(
        f_slot,
        m_slot,
        jnp.where(f_first, fa, ma),
        jnp.where(f_first, at_c3, mb),
        jnp.where(f_first, ma, fa),
        jnp.where(f_first, mb, at_c3),
    )
    return join(codes, own, arrived, width)


def solution(mesh):
    placed = (P("pipe", "section", None, "tp"), P("pipe", "section", None, "tp"), P(), P())
    return jax.shard_map(
        shards, mesh=mesh, in_specs=placed, out_specs=P("section", "tp", "pipe"), check_vma=False
    )
```

```python
import functools

import jax
import jax.numpy as jnp
from jax import lax
from jax.experimental import pallas as pl
from jax.experimental.pallas import tpu as pltpu
from jax.sharding import PartitionSpec as P

MIB = 1 << 20
LIMIT = 8 * MIB


def cost(micros):
    return pl.CostEstimate(flops=int(micros * 1.15e9), bytes_accessed=1, transcendentals=0)


def near_core(*arrays):
    return [pltpu.with_memory_space_constraint(array, pltpu.VMEM) for array in arrays]


SCALARS = pl.BlockSpec(memory_space=pltpu.SMEM)
HELD = pl.BlockSpec(memory_space=pltpu.VMEM)
ANYWHERE = pl.BlockSpec(memory_space=pl.ANY)


def tied(*values):
    return lax.optimization_barrier(values)


def after(value, *others):
    return tied(value, *others)[0]


def after_each(values, *others):
    return tied(*values, *others)[: len(values)]


def scalars(*values):
    return jnp.stack([jnp.asarray(v, jnp.int32) for v in values])


def turn_kernel(pick, *refs):
    refs, outs = refs[: len(refs) // 2], refs[len(refs) // 2 :]
    tile = refs[0].shape[1]
    rows = pl.program_id(0) * tile + lax.broadcasted_iota(jnp.int32, (tile, 1), 0)
    for x_ref, o_ref in zip(refs, outs):
        x = jnp.where(rows < pick[8], x_ref[0].astype(jnp.float32), 0.0)
        o_ref[...] = x.T.astype(o_ref.dtype)


def turn(pick, acts):
    _, tokens, feats = acts.shape
    tile, half = 256, feats // 2
    ins = [pl.BlockSpec((1, tile, half), functools.partial(lambda b, i, p: (p[b], i, p[4 + b]), b)) for b in range(4)]
    return pl.pallas_call(
        turn_kernel,
        grid_spec=pltpu.PrefetchScalarGridSpec(
            num_scalar_prefetch=1,
            grid=(tokens // tile,),
            in_specs=ins,
            out_specs=[pl.BlockSpec((half, tile), lambda i, p: (0, i))] * 4,
        ),
        out_shape=[pltpu.VMEM((half, tokens), acts.dtype)] * 4,
        compiler_params=pltpu.CompilerParams(vmem_limit_bytes=LIMIT),
        cost_estimate=cost(5),
    )(pick, *[acts] * 4)


def split(refs, counts):
    groups = []
    for count in counts:
        groups.append(refs[:count])
        refs = refs[count:]
    return groups, refs


def product(x_ref, kv_ref, slot):
    return jnp.dot(x_ref[...], kv_ref[slot], preferred_element_type=jnp.float32)


def send_kernel(counts, pick, *refs):
    xs, (groups, outs) = refs[:2], split(refs[2:], counts)
    width = groups[0][0].shape[2]
    for j, group in enumerate(groups):
        for code, kv_ref in enumerate(group):

            @pl.when(pick[2 + j] == code)
            def _():
                for step in range(2):
                    value = product(xs[step], kv_ref, pick[step])
                    outs[step][:, j * width : (j + 1) * width] = value.astype(outs[step].dtype)


def send_blocks(pick, xs, groups):
    half, _ = xs[0].shape
    width = groups[0][0].shape[2]
    flat = [array for group in groups for array in group]
    return pl.pallas_call(
        functools.partial(send_kernel, [len(group) for group in groups]),
        in_specs=[SCALARS] + [HELD] * (2 + len(flat)),
        out_specs=[HELD] * 2,
        out_shape=[pltpu.VMEM((half, len(groups) * width), xs[0].dtype)] * 2,
        compiler_params=pltpu.CompilerParams(vmem_limit_bytes=LIMIT),
        cost_estimate=cost(1.5 * len(groups)),
    )(pick, *near_core(*xs, *flat))


def choose_kernel(pick, *refs):
    for code in range(2):

        @pl.when(pick[0] == code)
        def _():
            for i in range(2):
                refs[4 + i][...] = refs[2 * i + code][...]


def choose(flag, first, second):
    array = first[0]
    return pl.pallas_call(
        choose_kernel,
        in_specs=[SCALARS] + [HELD] * 4,
        out_specs=[HELD] * 2,
        out_shape=[pltpu.VMEM(array.shape, array.dtype)] * 2,
        compiler_params=pltpu.CompilerParams(vmem_limit_bytes=LIMIT),
        cost_estimate=cost(0.5),
    )(flag, *near_core(*first, *second))


def place(pick, at, spot, out_ref, half, width):
    rows = pl.ds(pl.multiple_of(pick[at + 1] * half, half), half)
    cols = pl.ds(pl.multiple_of(spot * width, width), width)
    return out_ref.at[pick[at], rows, cols]


def own_kernel(counts, aliased, pick, *refs):
    xs, (groups, refs) = refs[:4], split(refs[4:], counts)
    arrived, (out_ref, late_ref, done, sems) = refs[:3], refs[3 + aliased :]
    half, width = done.shape[1:]
    heavy = pick[4] == 1
    base = 9
    for j, group in enumerate(groups):
        cols = slice(j * width, (j + 1) * width)
        for code, kv_ref in enumerate(group):
            here = pick[base + j] == code

            @pl.when(here & heavy)
            def _():
                for i in range(2):
                    value = product(xs[i], kv_ref, pick[5 + i]).astype(done.dtype)
                    done[2 * j + i] = value
                for i in range(2):
                    late_ref[i, :, cols] = product(xs[3 - i], kv_ref, pick[8 - i]).astype(done.dtype)

            @pl.when(here & jnp.logical_not(heavy))
            def _():
                for i in range(2):
                    late_ref[i, :, cols] = product(xs[1 - i], kv_ref, pick[6 - i]).astype(done.dtype)

        @pl.when(jnp.logical_not(heavy))
        def _():
            for i in range(2):
                done[2 * j + i] = jnp.zeros(done.shape[1:], done.dtype)

        for i in range(2):
            for choice, ref in enumerate(arrived):

                @pl.when(heavy & (pick[base + len(counts) + i] == choice))
                def _():
                    total = done[2 * j + i].astype(jnp.float32) + ref[:, cols].astype(jnp.float32)
                    done[2 * j + i] = total.astype(done.dtype)

            spot = pick[base + len(counts) + 2 + j]
            pltpu.make_async_copy(done.at[2 * j + i], place(pick, 2 * i, spot, out_ref, half, width), sems.at[2 * j + i]).start()

    for j in range(len(groups)):
        for i in range(2):
            spot = pick[base + len(counts) + 2 + j]
            pltpu.make_async_copy(done.at[2 * j + i], place(pick, 2 * i, spot, out_ref, half, width), sems.at[2 * j + i]).wait()


def own_blocks(pick, xs, groups, arrived, out_cols, before):
    half, _ = xs[0].shape
    dtype = xs[0].dtype
    width = groups[0][0].shape[2]
    counts = [len(group) for group in groups]
    flat = [array for group in groups for array in group]
    held = [] if before is None else [before]
    return pl.pallas_call(
        functools.partial(own_kernel, counts, len(held)),
        in_specs=[SCALARS] + [HELD] * (4 + len(flat) + len(arrived)) + [ANYWHERE] * len(held),
        out_specs=[ANYWHERE, HELD],
        out_shape=[
            jax.ShapeDtypeStruct((2, 2 * half, out_cols), dtype),
            pltpu.VMEM((2, half, len(groups) * width), dtype),
        ],
        input_output_aliases={5 + len(flat) + len(arrived): 0} if held else {},
        scratch_shapes=[
            pltpu.VMEM((2 * len(groups), half, width), dtype),
            pltpu.SemaphoreType.DMA((2 * len(groups),)),
        ],
        compiler_params=pltpu.CompilerParams(vmem_limit_bytes=LIMIT),
        cost_estimate=cost(2.5 * len(groups)),
    )(pick, *near_core(*xs, *flat, *arrived), *held)


def late_kernel(sets, width, pick, *refs):
    blocks = [refs[4 * k : 4 * k + 4] for k in range(len(sets))]
    out_ref, done, sems = refs[4 * len(sets) + 1 :]
    half = done.shape[1]
    copies = []
    for k, places in enumerate(sets):
        own_ref, c3_ref, i3_ref, c2_ref = blocks[k]
        for j in range(places):
            cols = slice(j * width, (j + 1) * width)
            n = len(copies)

            def put(row, ref):
                total = own_ref[row, :, cols].astype(jnp.float32) + ref[:, cols].astype(jnp.float32)
                done[n + row] = total.astype(done.dtype)

            put(0, c3_ref)
            for code, ref in enumerate((c2_ref, i3_ref)):

                @pl.when(pick[4] == code)
                def _():
                    put(1, ref)

            for row in range(2):
                to = place(pick, 2 * row, pick[5 + n // 2], out_ref, half, width)
                copies.append(pltpu.make_async_copy(done.at[n + row], to, sems.at[n + row]))
                copies[-1].start()
    for copy in copies:
        copy.wait()


def late_blocks(pick, out, owns, arrived, width):
    half = arrived[0][0].shape[0]
    sets = [blocks[0].shape[1] // width for blocks in arrived]
    flat = [block for own, blocks in zip(owns, arrived) for block in (own, *blocks)]
    count = 2 * sum(sets)
    return pl.pallas_call(
        functools.partial(late_kernel, sets, width),
        in_specs=[SCALARS] + [HELD] * len(flat) + [ANYWHERE],
        out_specs=ANYWHERE,
        out_shape=jax.ShapeDtypeStruct(out.shape, out.dtype),
        input_output_aliases={1 + len(flat): 0},
        scratch_shapes=[pltpu.VMEM((count, half, width), out.dtype), pltpu.SemaphoreType.DMA((count,))],
        compiler_params=pltpu.CompilerParams(vmem_limit_bytes=LIMIT),
        cost_estimate=cost(2),
    )(pick, *near_core(*flat), out)


def shards(acts, kv_grads, layer_section, token_counts):
    sections = lax.axis_size("section")
    chips = lax.axis_size("tp") // 2
    pipe = lax.axis_index("pipe")
    section = lax.axis_index("section")
    z, core = lax.axis_index("tp") // 2, lax.axis_index("tp") % 2
    acts, kv = acts[0], kv_grads[0]
    width = kv.shape[2]
    counts = jnp.sum((layer_section == section).astype(jnp.int32), axis=1)
    own_count = lax.dynamic_index_in_dim(counts, pipe, 0, keepdims=False)
    other_count = lax.dynamic_index_in_dim(counts, 1 - pipe, 0, keepdims=False)
    heavy = own_count == 2
    matched = own_count == other_count
    limit = lax.dynamic_index_in_dim(token_counts, pipe, 0, keepdims=False)
    h = heavy.astype(jnp.int32)
    f_slot = jnp.where(heavy, section % 2, 0)
    m_slot = 1 - f_slot

    def across(array, name):
        pairs = [
            (p * sections + s, (1 - p) * sections + (s ^ 1)) for p in range(2) for s in range(sections)
        ]
        with jax.named_scope(name):
            return lax.ppermute(array, ("pipe", "section"), pairs)

    def beside(array, name):
        with jax.named_scope(name):
            return lax.ppermute(array, "section", [(s, s ^ 1) for s in range(sections)])

    def swapped(array, name):
        with jax.named_scope(name):
            return lax.ppermute(array, "tp", [(t, t ^ 1) for t in range(2 * chips)])

    def around(array, by, name):
        pairs = [(2 * i + c, (i + (by if c == 0 else -by)) % chips * 2 + c) for i in range(chips) for c in range(2)]
        with jax.named_scope(name):
            return lax.ppermute(array, "tp", pairs)

    def codes_of(relay):
        inside = z // 2 == 1 - relay
        even, same = z % 2 == 0, z % 2 == core
        pick = jnp.where
        codes = (
            pick(inside, 0, pick(same, 1, 2)),
            pick(inside, 0, 1),
            pick(inside, pick(same, 1, 0), 2),
            pick(inside == same, 0, 1),
        )
        up, down, far = (z + 1) % chips, (z + chips - 1) % chips, (z + 2) % chips
        sources = (
            pick(inside, z * 2 + core, pick(even, down * 2, up * 2 + 1)),
            pick(inside, z * 2 + 1 - core, far * 2 + core),
            pick(inside, pick(even, up * 2 + 1, down * 2), far * 2 + 1 - core),
            pick(inside == even, up * 2, down * 2 + 1),
        )
        return codes, sources

    slot_of = lambda role: jnp.where(role == 1, m_slot, f_slot)
    sent_codes, _ = codes_of(pipe)
    kept_codes, kept_sources = codes_of(1 - pipe)
    places = [source - pipe * chips for source in kept_sources]
    parts = ((0,), (1, 2), (3,))
    at_c1, at_c2, at_i2 = range(3)
    pick = functools.partial(jnp.where, heavy)
    roles = (pick(1, 0), 0, 1, pick(0, 1))
    halves = (0, pick(0, 1), pick(1, 0), 1)
    slots = tuple(slot_of(role) for role in roles)
    early = (jnp.where(matched, at_i2, at_c1), jnp.where(matched, at_c2, at_i2))
    early_to = (m_slot, 0, pick(f_slot, m_slot), pick(0, 1))
    late_to = (f_slot, 1, pick(m_slot, f_slot), h)
    sent, kept = [], []
    for part in parts:
        codes = [sent_codes[j] for j in part]
        sent += [scalars(*slots[:2], *codes), scalars(*slots[2:], *codes)]
        codes, spots = [kept_codes[j] for j in part], [places[j] for j in part]
        kept.append(scalars(*early_to, h, *slots, *codes, *early, *spots))
    last = scalars(*late_to, matched, *places)
    flag, turns, last, *sent = tied(scalars(1 - h), scalars(*slots, *halves, limit), last, *sent, *kept)
    sent, kept = sent[: 2 * len(parts)], sent[2 * len(parts) :]

    with jax.named_scope("turned"):
        turned = turn(turns, acts)

    def first_step(k, groups):
        with jax.named_scope(f"first_{k}"):
            c1, i1 = send_blocks(sent[2 * k], turned[:2], groups)
        pick2, c1, i1 = tied(sent[2 * k + 1], c1, i1)
        with jax.named_scope(f"second_{k}"):
            x2, s2 = send_blocks(pick2, turned[2:], groups)
        return across(c1, f"rc1_{k}"), beside(i1, f"ri1_{k}"), x2, s2

    def second_step(rc1, ri1, x2, s2):
        with jax.named_scope("chosen2"):
            return choose(flag, (x2, ri1), (s2, rc1))

    def third_step(rc1, ri1, rc2, ri2):
        with jax.named_scope("chosen3"):
            return choose(flag, (ri1, ri2), (rc1, rc2))

    def keep(k, groups, arrived, before):
        with jax.named_scope(f"kept_{k}"):
            return own_blocks(kept[k], turned, groups, arrived, chips * width, before)

    def finish(out, owns, arrived):
        with jax.named_scope("joined"):
            return late_blocks(last, out, owns, arrived, width)

    near, pair, *turned = tied(around(kv, 1, "near"), swapped(kv, "pair"), *turned)
    far = around(near, 1, "far")
    near_pair = swapped(near, "near_pair")
    set0 = [[kv, near, near_pair]]
    rc1_0, ri1_0, x2_0, s2_0 = first_step(0, set0)
    c2_0, i2_0 = second_step(rc1_0, ri1_0, x2_0, s2_0)
    rc2_0 = across(c2_0, "rc2_0")
    ri2_0 = beside(i2_0, "ri2_0")
    c3_0, i3_0 = third_step(rc1_0, ri1_0, rc2_0, ri2_0)
    rc3_0 = across(c3_0, "rc3_0")
    ri3_0 = beside(i3_0, "ri3_0")
    far = after(far, c3_0, i3_0)
    late = around(after(kv, far), -1, "late")
    far_pair = swapped(far, "far_pair")
    set1 = [[pair, far], [near, near_pair, far_pair]]
    rc1_1, ri1_1, x2_1, s2_1 = first_step(1, set1)
    out, own_0 = keep(0, set0, (rc1_0, rc2_0, ri2_0), None)
    c2_1, i2_1 = second_step(rc1_1, ri1_1, x2_1, s2_1)
    late = after(late, c2_1, i2_1)
    late_pair = swapped(late, "late_pair")
    rc3_0, ri3_0, late_pair = tied(rc3_0, ri3_0, late_pair)
    set2 = [[late, late_pair]]
    rc1_2, ri1_2, x2_2, s2_2 = first_step(2, set2)
    rc2_1 = across(c2_1, "rc2_1")
    ri2_1 = beside(i2_1, "ri2_1")
    c2_2, i2_2 = second_step(rc1_2, ri1_2, x2_2, s2_2)
    rc2_2 = across(c2_2, "rc2_2")
    ri2_2 = beside(i2_2, "ri2_2")
    c3_1, i3_1 = third_step(rc1_1, ri1_1, rc2_1, ri2_1)
    rc3_1 = across(c3_1, "rc3_1")
    ri3_1 = beside(i3_1, "ri3_1")
    out, own_1 = keep(1, set1, (rc1_1, rc2_1, ri2_1), out)
    c3_2, i3_2 = third_step(rc1_2, ri1_2, rc2_2, ri2_2)
    rc3_2 = across(c3_2, "rc3_2")
    ri3_2 = beside(i3_2, "ri3_2")
    out, own_2 = keep(2, set2, (rc1_2, rc2_2, ri2_2), out)
    arrived = ((rc3_0, ri3_0, rc2_0), (rc3_1, ri3_1, rc2_1), (rc3_2, ri3_2, rc2_2))
    return finish(out, (own_0, own_1, own_2), arrived)


def solution(mesh):
    placed = (P("pipe", "section", None, "tp"), P("pipe", "section", None, "tp"), P(), P())
    return jax.shard_map(
        shards, mesh=mesh, in_specs=placed, out_specs=P("section", "tp", "pipe"), check_vma=False
    )
```

```python
import functools

import jax
import jax.numpy as jnp
from jax import lax
from jax.experimental import pallas as pl
from jax.experimental.pallas import tpu as pltpu
from jax.sharding import PartitionSpec as P

MIB = 1 << 20
LIMIT = 8 * MIB


def cost(micros):
    return pl.CostEstimate(flops=int(micros * 1.15e9), bytes_accessed=1, transcendentals=0)


def near_core(*arrays):
    return [pltpu.with_memory_space_constraint(array, pltpu.VMEM) for array in arrays]


SCALARS = pl.BlockSpec(memory_space=pltpu.SMEM)
HELD = pl.BlockSpec(memory_space=pltpu.VMEM)
ANYWHERE = pl.BlockSpec(memory_space=pl.ANY)


def tied(*values):
    return lax.optimization_barrier(values)


def after(value, *others):
    return tied(value, *others)[0]


def after_each(values, *others):
    return tied(*values, *others)[: len(values)]


def scalars(*values):
    return jnp.stack([jnp.asarray(v, jnp.int32) for v in values])


def turn_kernel(pick, *refs):
    refs, outs = refs[: len(refs) // 2], refs[len(refs) // 2 :]
    tile = refs[0].shape[1]
    rows = pl.program_id(0) * tile + lax.broadcasted_iota(jnp.int32, (tile, 1), 0)
    for x_ref, o_ref in zip(refs, outs):
        x = jnp.where(rows < pick[8], x_ref[0].astype(jnp.float32), 0.0)
        o_ref[...] = x.T.astype(o_ref.dtype)


def turn(pick, acts):
    _, tokens, feats = acts.shape
    tile, half = 256, feats // 2
    ins = [pl.BlockSpec((1, tile, half), functools.partial(lambda b, i, p: (p[b], i, p[4 + b]), b)) for b in range(4)]
    return pl.pallas_call(
        turn_kernel,
        grid_spec=pltpu.PrefetchScalarGridSpec(
            num_scalar_prefetch=1,
            grid=(tokens // tile,),
            in_specs=ins,
            out_specs=[pl.BlockSpec((half, tile), lambda i, p: (0, i))] * 4,
        ),
        out_shape=[pltpu.VMEM((half, tokens), acts.dtype)] * 4,
        compiler_params=pltpu.CompilerParams(vmem_limit_bytes=LIMIT),
        cost_estimate=cost(5),
    )(pick, *[acts] * 4)


def split(refs, counts):
    groups = []
    for count in counts:
        groups.append(refs[:count])
        refs = refs[count:]
    return groups, refs


def product(x_ref, kv_ref, slot):
    return jnp.dot(x_ref[...], kv_ref[slot], preferred_element_type=jnp.float32)


def send_kernel(counts, pick, *refs):
    xs, (groups, outs) = refs[:2], split(refs[2:], counts)
    width = groups[0][0].shape[2]
    for j, group in enumerate(groups):
        for code, kv_ref in enumerate(group):

            @pl.when(pick[2 + j] == code)
            def _():
                for step in range(2):
                    value = product(xs[step], kv_ref, pick[step])
                    outs[step][:, j * width : (j + 1) * width] = value.astype(outs[step].dtype)


def send_blocks(pick, xs, groups):
    half, _ = xs[0].shape
    width = groups[0][0].shape[2]
    flat = [array for group in groups for array in group]
    return pl.pallas_call(
        functools.partial(send_kernel, [len(group) for group in groups]),
        in_specs=[SCALARS] + [HELD] * (2 + len(flat)),
        out_specs=[HELD] * 2,
        out_shape=[pltpu.VMEM((half, len(groups) * width), xs[0].dtype)] * 2,
        compiler_params=pltpu.CompilerParams(vmem_limit_bytes=LIMIT),
        cost_estimate=cost(1.5 * len(groups)),
    )(pick, *near_core(*xs, *flat))


def choose_kernel(pick, *refs):
    for code in range(2):

        @pl.when(pick[0] == code)
        def _():
            for i in range(2):
                refs[4 + i][...] = refs[2 * i + code][...]


def choose(flag, first, second):
    array = first[0]
    return pl.pallas_call(
        choose_kernel,
        in_specs=[SCALARS] + [HELD] * 4,
        out_specs=[HELD] * 2,
        out_shape=[pltpu.VMEM(array.shape, array.dtype)] * 2,
        compiler_params=pltpu.CompilerParams(vmem_limit_bytes=LIMIT),
        cost_estimate=cost(0.5),
    )(flag, *near_core(*first, *second))


def place(pick, at, spot, out_ref, half, width):
    rows = pl.ds(pl.multiple_of(pick[at + 1] * half, half), half)
    cols = pl.ds(pl.multiple_of(spot * width, width), width)
    return out_ref.at[pick[at], rows, cols]


def own_kernel(counts, aliased, pick, *refs):
    xs, (groups, refs) = refs[:4], split(refs[4:], counts)
    arrived, (out_ref, late_ref, done, sems) = refs[:3], refs[3 + aliased :]
    half, width = done.shape[1:]
    heavy = pick[4] == 1
    base = 9
    for j, group in enumerate(groups):
        cols = slice(j * width, (j + 1) * width)
        for code, kv_ref in enumerate(group):
            here = pick[base + j] == code

            @pl.when(here & heavy)
            def _():
                for i in range(2):
                    value = product(xs[i], kv_ref, pick[5 + i]).astype(done.dtype)
                    done[2 * j + i] = value
                for i in range(2):
                    late_ref[i, :, cols] = product(xs[3 - i], kv_ref, pick[8 - i]).astype(done.dtype)

            @pl.when(here & jnp.logical_not(heavy))
            def _():
                for i in range(2):
                    late_ref[i, :, cols] = product(xs[1 - i], kv_ref, pick[6 - i]).astype(done.dtype)

        @pl.when(jnp.logical_not(heavy))
        def _():
            for i in range(2):
                done[2 * j + i] = jnp.zeros(done.shape[1:], done.dtype)

        for i in range(2):
            for choice, ref in enumerate(arrived):

                @pl.when(heavy & (pick[base + len(counts) + i] == choice))
                def _():
                    total = done[2 * j + i].astype(jnp.float32) + ref[:, cols].astype(jnp.float32)
                    done[2 * j + i] = total.astype(done.dtype)

            spot = pick[base + len(counts) + 2 + j]
            pltpu.make_async_copy(done.at[2 * j + i], place(pick, 2 * i, spot, out_ref, half, width), sems.at[2 * j + i]).start()

    for j in range(len(groups)):
        for i in range(2):
            spot = pick[base + len(counts) + 2 + j]
            pltpu.make_async_copy(done.at[2 * j + i], place(pick, 2 * i, spot, out_ref, half, width), sems.at[2 * j + i]).wait()


def own_blocks(pick, xs, groups, arrived, out_cols, before):
    half, _ = xs[0].shape
    dtype = xs[0].dtype
    width = groups[0][0].shape[2]
    counts = [len(group) for group in groups]
    flat = [array for group in groups for array in group]
    held = [] if before is None else [before]
    return pl.pallas_call(
        functools.partial(own_kernel, counts, len(held)),
        in_specs=[SCALARS] + [HELD] * (4 + len(flat) + len(arrived)) + [ANYWHERE] * len(held),
        out_specs=[ANYWHERE, HELD],
        out_shape=[
            jax.ShapeDtypeStruct((2, 2 * half, out_cols), dtype),
            pltpu.VMEM((2, half, len(groups) * width), dtype),
        ],
        input_output_aliases={5 + len(flat) + len(arrived): 0} if held else {},
        scratch_shapes=[
            pltpu.VMEM((2 * len(groups), half, width), dtype),
            pltpu.SemaphoreType.DMA((2 * len(groups),)),
        ],
        compiler_params=pltpu.CompilerParams(vmem_limit_bytes=LIMIT),
        cost_estimate=cost(2.5 * len(groups)),
    )(pick, *near_core(*xs, *flat, *arrived), *held)


def late_kernel(sets, width, pick, *refs):
    blocks = [refs[4 * k : 4 * k + 4] for k in range(len(sets))]
    out_ref, done, sems = refs[4 * len(sets) + 1 :]
    half = done.shape[1]
    copies = []
    for k, places in enumerate(sets):
        own_ref, c3_ref, i3_ref, c2_ref = blocks[k]
        for j in range(places):
            cols = slice(j * width, (j + 1) * width)
            n = len(copies)

            def put(row, ref):
                total = own_ref[row, :, cols].astype(jnp.float32) + ref[:, cols].astype(jnp.float32)
                done[n + row] = total.astype(done.dtype)

            put(0, c3_ref)
            for code, ref in enumerate((c2_ref, i3_ref)):

                @pl.when(pick[4] == code)
                def _():
                    put(1, ref)

            for row in range(2):
                to = place(pick, 2 * row, pick[5 + n // 2], out_ref, half, width)
                copies.append(pltpu.make_async_copy(done.at[n + row], to, sems.at[n + row]))
                copies[-1].start()
    for copy in copies:
        copy.wait()


def late_blocks(pick, out, owns, arrived, width):
    half = arrived[0][0].shape[0]
    sets = [blocks[0].shape[1] // width for blocks in arrived]
    flat = [block for own, blocks in zip(owns, arrived) for block in (own, *blocks)]
    count = 2 * sum(sets)
    return pl.pallas_call(
        functools.partial(late_kernel, sets, width),
        in_specs=[SCALARS] + [HELD] * len(flat) + [ANYWHERE],
        out_specs=ANYWHERE,
        out_shape=jax.ShapeDtypeStruct(out.shape, out.dtype),
        input_output_aliases={1 + len(flat): 0},
        scratch_shapes=[pltpu.VMEM((count, half, width), out.dtype), pltpu.SemaphoreType.DMA((count,))],
        compiler_params=pltpu.CompilerParams(vmem_limit_bytes=LIMIT),
        cost_estimate=cost(2),
    )(pick, *near_core(*flat), out)


def shards(acts, kv_grads, layer_section, token_counts):
    sections = lax.axis_size("section")
    chips = lax.axis_size("tp") // 2
    pipe = lax.axis_index("pipe")
    section = lax.axis_index("section")
    z, core = lax.axis_index("tp") // 2, lax.axis_index("tp") % 2
    acts, kv = acts[0], kv_grads[0]
    width = kv.shape[2]
    counts = jnp.sum((layer_section == section).astype(jnp.int32), axis=1)
    own_count = lax.dynamic_index_in_dim(counts, pipe, 0, keepdims=False)
    other_count = lax.dynamic_index_in_dim(counts, 1 - pipe, 0, keepdims=False)
    heavy = own_count == 2
    matched = own_count == other_count
    limit = lax.dynamic_index_in_dim(token_counts, pipe, 0, keepdims=False)
    h = heavy.astype(jnp.int32)
    f_slot = jnp.where(heavy, section % 2, 0)
    m_slot = 1 - f_slot

    def across(array, name):
        pairs = [
            (p * sections + s, (1 - p) * sections + (s ^ 1)) for p in range(2) for s in range(sections)
        ]
        with jax.named_scope(name):
            return lax.ppermute(array, ("pipe", "section"), pairs)

    def beside(array, name):
        with jax.named_scope(name):
            return lax.ppermute(array, "section", [(s, s ^ 1) for s in range(sections)])

    def swapped(array, name):
        with jax.named_scope(name):
            return lax.ppermute(array, "tp", [(t, t ^ 1) for t in range(2 * chips)])

    def around(array, by, name):
        pairs = [(2 * i + c, (i + (by if c == 0 else -by)) % chips * 2 + c) for i in range(chips) for c in range(2)]
        with jax.named_scope(name):
            return lax.ppermute(array, "tp", pairs)

    def codes_of(relay):
        inside = z // 2 == 1 - relay
        even, same = z % 2 == 0, z % 2 == core
        pick = jnp.where
        codes = (
            pick(inside, 0, pick(same, 1, 2)),
            pick(inside, 0, 1),
            pick(inside, pick(same, 1, 0), 2),
            pick(inside == same, 0, 1),
        )
        up, down, far = (z + 1) % chips, (z + chips - 1) % chips, (z + 2) % chips
        sources = (
            pick(inside, z * 2 + core, pick(even, down * 2, up * 2 + 1)),
            pick(inside, z * 2 + 1 - core, far * 2 + core),
            pick(inside, pick(even, up * 2 + 1, down * 2), far * 2 + 1 - core),
            pick(inside == even, up * 2, down * 2 + 1),
        )
        return codes, sources

    slot_of = lambda role: jnp.where(role == 1, m_slot, f_slot)
    sent_codes, _ = codes_of(pipe)
    kept_codes, kept_sources = codes_of(1 - pipe)
    places = [source - pipe * chips for source in kept_sources]
    parts = ((0,), (1, 2), (3,))
    at_c1, at_c2, at_i2 = range(3)
    pick = functools.partial(jnp.where, heavy)
    roles = (pick(1, 0), 0, 1, pick(0, 1))
    halves = (0, pick(0, 1), pick(1, 0), 1)
    slots = tuple(slot_of(role) for role in roles)
    early = (jnp.where(matched, at_i2, at_c1), jnp.where(matched, at_c2, at_i2))
    early_to = (m_slot, 0, pick(f_slot, m_slot), pick(0, 1))
    late_to = (f_slot, 1, pick(m_slot, f_slot), h)
    sent, kept = [], []
    for part in parts:
        codes = [sent_codes[j] for j in part]
        sent += [scalars(*slots[:2], *codes), scalars(*slots[2:], *codes)]
        codes, spots = [kept_codes[j] for j in part], [places[j] for j in part]
        kept.append(scalars(*early_to, h, *slots, *codes, *early, *spots))
    last = scalars(*late_to, matched, *places)
    flag, turns, last, *sent = tied(scalars(1 - h), scalars(*slots, *halves, limit), last, *sent, *kept)
    sent, kept = sent[: 2 * len(parts)], sent[2 * len(parts) :]

    with jax.named_scope("turned"):
        turned = turn(turns, acts)

    def first_step(k, groups):
        with jax.named_scope(f"first_{k}"):
            c1, i1 = send_blocks(sent[2 * k], turned[:2], groups)
        pick2, c1, i1 = tied(sent[2 * k + 1], c1, i1)
        with jax.named_scope(f"second_{k}"):
            x2, s2 = send_blocks(pick2, turned[2:], groups)
        return across(c1, f"rc1_{k}"), beside(i1, f"ri1_{k}"), x2, s2

    def second_step(rc1, ri1, x2, s2):
        with jax.named_scope("chosen2"):
            return choose(flag, (x2, ri1), (s2, rc1))

    def third_step(rc1, ri1, rc2, ri2):
        with jax.named_scope("chosen3"):
            return choose(flag, (ri1, ri2), (rc1, rc2))

    def keep(k, groups, arrived, before):
        with jax.named_scope(f"kept_{k}"):
            return own_blocks(kept[k], turned, groups, arrived, chips * width, before)

    def finish(out, owns, arrived):
        with jax.named_scope("joined"):
            return late_blocks(last, out, owns, arrived, width)

    near, pair, *turned = tied(around(kv, 1, "near"), swapped(kv, "pair"), *turned)
    far = around(near, 1, "far")
    near_pair = swapped(near, "near_pair")
    set0 = [[kv, near, near_pair]]
    rc1_0, ri1_0, x2_0, s2_0 = first_step(0, set0)
    c2_0, i2_0 = second_step(rc1_0, ri1_0, x2_0, s2_0)
    rc2_0 = across(c2_0, "rc2_0")
    ri2_0 = beside(i2_0, "ri2_0")
    c3_0, i3_0 = third_step(rc1_0, ri1_0, rc2_0, ri2_0)
    rc3_0 = across(c3_0, "rc3_0")
    ri3_0 = beside(i3_0, "ri3_0")
    far = after(far, c3_0, i3_0)
    late = around(after(kv, far), -1, "late")
    far_pair = swapped(far, "far_pair")
    set1 = [[pair, far], [near, near_pair, far_pair]]
    rc1_1, ri1_1, x2_1, s2_1 = first_step(1, set1)
    out, own_0 = keep(0, set0, (rc1_0, rc2_0, ri2_0), None)
    rc3_0, ri3_0, own_0, rc1_1, ri1_1 = tied(rc3_0, ri3_0, own_0, rc1_1, ri1_1)
    c2_1, i2_1 = second_step(rc1_1, ri1_1, x2_1, s2_1)
    late = after(late, c2_1, i2_1)
    late_pair = swapped(late, "late_pair")
    set2 = [[late, late_pair]]
    rc1_2, ri1_2, x2_2, s2_2 = first_step(2, set2)
    rc2_1 = across(c2_1, "rc2_1")
    ri2_1 = beside(i2_1, "ri2_1")
    c2_2, i2_2 = second_step(rc1_2, ri1_2, x2_2, s2_2)
    rc2_2 = across(c2_2, "rc2_2")
    ri2_2 = beside(i2_2, "ri2_2")
    c3_1, i3_1 = third_step(rc1_1, ri1_1, rc2_1, ri2_1)
    rc3_1 = across(c3_1, "rc3_1")
    ri3_1 = beside(i3_1, "ri3_1")
    out, own_1 = keep(1, set1, (rc1_1, rc2_1, ri2_1), out)
    c3_2, i3_2 = third_step(rc1_2, ri1_2, rc2_2, ri2_2)
    rc3_2 = across(c3_2, "rc3_2")
    ri3_2 = beside(i3_2, "ri3_2")
    out, own_2 = keep(2, set2, (rc1_2, rc2_2, ri2_2), out)
    arrived = ((rc3_0, ri3_0, rc2_0), (rc3_1, ri3_1, rc2_1), (rc3_2, ri3_2, rc2_2))
    return finish(out, (own_0, own_1, own_2), arrived)


def solution(mesh):
    placed = (P("pipe", "section", None, "tp"), P("pipe", "section", None, "tp"), P(), P())
    return jax.shard_map(
        shards, mesh=mesh, in_specs=placed, out_specs=P("section", "tp", "pipe"), check_vma=False
    )
```

```python
import functools

import jax
import jax.numpy as jnp
from jax import lax
from jax.experimental import pallas as pl
from jax.experimental.pallas import tpu as pltpu
from jax.sharding import PartitionSpec as P

MIB = 1 << 20
LIMIT = 8 * MIB


def cost(micros):
    return pl.CostEstimate(flops=int(micros * 1.15e9), bytes_accessed=1, transcendentals=0)


def near_core(*arrays):
    return [pltpu.with_memory_space_constraint(array, pltpu.VMEM) for array in arrays]


SCALARS = pl.BlockSpec(memory_space=pltpu.SMEM)
HELD = pl.BlockSpec(memory_space=pltpu.VMEM)
ANYWHERE = pl.BlockSpec(memory_space=pl.ANY)


def tied(*values):
    return lax.optimization_barrier(values)


def after(value, *others):
    return tied(value, *others)[0]


def after_each(values, *others):
    return tied(*values, *others)[: len(values)]


def scalars(*values):
    return jnp.stack([jnp.asarray(v, jnp.int32) for v in values])


def turn_kernel(pick, *refs):
    refs, outs = refs[: len(refs) // 2], refs[len(refs) // 2 :]
    tile = refs[0].shape[1]
    rows = pl.program_id(0) * tile + lax.broadcasted_iota(jnp.int32, (tile, 1), 0)
    for x_ref, o_ref in zip(refs, outs):
        x = jnp.where(rows < pick[8], x_ref[0].astype(jnp.float32), 0.0)
        o_ref[...] = x.T.astype(o_ref.dtype)


def turn(pick, acts):
    _, tokens, feats = acts.shape
    tile, half = 256, feats // 2
    ins = [pl.BlockSpec((1, tile, half), functools.partial(lambda b, i, p: (p[b], i, p[4 + b]), b)) for b in range(4)]
    return pl.pallas_call(
        turn_kernel,
        grid_spec=pltpu.PrefetchScalarGridSpec(
            num_scalar_prefetch=1,
            grid=(tokens // tile,),
            in_specs=ins,
            out_specs=[pl.BlockSpec((half, tile), lambda i, p: (0, i))] * 4,
        ),
        out_shape=[pltpu.VMEM((half, tokens), acts.dtype)] * 4,
        compiler_params=pltpu.CompilerParams(vmem_limit_bytes=LIMIT),
        cost_estimate=cost(5),
    )(pick, *[acts] * 4)


def split(refs, counts):
    groups = []
    for count in counts:
        groups.append(refs[:count])
        refs = refs[count:]
    return groups, refs


def product(x_ref, kv_ref, slot):
    return jnp.dot(x_ref[...], kv_ref[slot], preferred_element_type=jnp.float32)


def send_kernel(counts, pick, *refs):
    xs, (groups, outs) = refs[:2], split(refs[2:], counts)
    width = groups[0][0].shape[2]
    for j, group in enumerate(groups):
        for code, kv_ref in enumerate(group):

            @pl.when(pick[2 + j] == code)
            def _():
                for step in range(2):
                    value = product(xs[step], kv_ref, pick[step])
                    outs[step][:, j * width : (j + 1) * width] = value.astype(outs[step].dtype)


def send_blocks(pick, xs, groups):
    half, _ = xs[0].shape
    width = groups[0][0].shape[2]
    flat = [array for group in groups for array in group]
    return pl.pallas_call(
        functools.partial(send_kernel, [len(group) for group in groups]),
        in_specs=[SCALARS] + [HELD] * (2 + len(flat)),
        out_specs=[HELD] * 2,
        out_shape=[pltpu.VMEM((half, len(groups) * width), xs[0].dtype)] * 2,
        compiler_params=pltpu.CompilerParams(vmem_limit_bytes=LIMIT),
        cost_estimate=cost(1.5 * len(groups)),
    )(pick, *near_core(*xs, *flat))


def choose_kernel(pieces, pick, *refs):
    width = refs[4].shape[1]
    for code in range(2):

        @pl.when(pick[0] == code)
        def _():
            for n, out_ref in enumerate(refs[4:]):
                at = n % pieces * width
                out_ref[...] = refs[2 * (n // pieces) + code][:, at : at + width]


def choose(flag, first, second, pieces=1):
    rows, cols = first[0].shape
    return pl.pallas_call(
        functools.partial(choose_kernel, pieces),
        in_specs=[SCALARS] + [HELD] * 4,
        out_specs=[HELD] * (2 * pieces),
        out_shape=[pltpu.VMEM((rows, cols // pieces), first[0].dtype)] * (2 * pieces),
        compiler_params=pltpu.CompilerParams(vmem_limit_bytes=LIMIT),
        cost_estimate=cost(0.5),
    )(flag, *near_core(*first, *second))


def place(pick, at, spot, out_ref, half, width):
    rows = pl.ds(pl.multiple_of(pick[at + 1] * half, half), half)
    cols = pl.ds(pl.multiple_of(spot * width, width), width)
    return out_ref.at[pick[at], rows, cols]


def own_kernel(counts, aliased, pick, *refs):
    xs, (groups, refs) = refs[:4], split(refs[4:], counts)
    arrived, (out_ref, late_ref, done, sems) = refs[:3], refs[3 + aliased :]
    half, width = done.shape[1:]
    heavy = pick[4] == 1
    base = 9
    for j, group in enumerate(groups):
        cols = slice(j * width, (j + 1) * width)
        for code, kv_ref in enumerate(group):
            here = pick[base + j] == code

            @pl.when(here & heavy)
            def _():
                for i in range(2):
                    value = product(xs[i], kv_ref, pick[5 + i]).astype(done.dtype)
                    done[2 * j + i] = value
                for i in range(2):
                    late_ref[i, :, cols] = product(xs[3 - i], kv_ref, pick[8 - i]).astype(done.dtype)

            @pl.when(here & jnp.logical_not(heavy))
            def _():
                for i in range(2):
                    late_ref[i, :, cols] = product(xs[1 - i], kv_ref, pick[6 - i]).astype(done.dtype)

        @pl.when(jnp.logical_not(heavy))
        def _():
            for i in range(2):
                done[2 * j + i] = jnp.zeros(done.shape[1:], done.dtype)

        for i in range(2):
            for choice, ref in enumerate(arrived):

                @pl.when(heavy & (pick[base + len(counts) + i] == choice))
                def _():
                    total = done[2 * j + i].astype(jnp.float32) + ref[:, cols].astype(jnp.float32)
                    done[2 * j + i] = total.astype(done.dtype)

            spot = pick[base + len(counts) + 2 + j]
            pltpu.make_async_copy(done.at[2 * j + i], place(pick, 2 * i, spot, out_ref, half, width), sems.at[2 * j + i]).start()

    for j in range(len(groups)):
        for i in range(2):
            spot = pick[base + len(counts) + 2 + j]
            pltpu.make_async_copy(done.at[2 * j + i], place(pick, 2 * i, spot, out_ref, half, width), sems.at[2 * j + i]).wait()


def own_blocks(pick, xs, groups, arrived, out_cols, before):
    half, _ = xs[0].shape
    dtype = xs[0].dtype
    width = groups[0][0].shape[2]
    counts = [len(group) for group in groups]
    flat = [array for group in groups for array in group]
    held = [] if before is None else [before]
    return pl.pallas_call(
        functools.partial(own_kernel, counts, len(held)),
        in_specs=[SCALARS] + [HELD] * (4 + len(flat) + len(arrived)) + [ANYWHERE] * len(held),
        out_specs=[ANYWHERE, HELD],
        out_shape=[
            jax.ShapeDtypeStruct((2, 2 * half, out_cols), dtype),
            pltpu.VMEM((2, half, len(groups) * width), dtype),
        ],
        input_output_aliases={5 + len(flat) + len(arrived): 0} if held else {},
        scratch_shapes=[
            pltpu.VMEM((2 * len(groups), half, width), dtype),
            pltpu.SemaphoreType.DMA((2 * len(groups),)),
        ],
        compiler_params=pltpu.CompilerParams(vmem_limit_bytes=LIMIT),
        cost_estimate=cost(2.5 * len(groups)),
    )(pick, *near_core(*xs, *flat, *arrived), *held)


def late_kernel(sets, width, pick, *refs):
    blocks = []
    for places in sets:
        blocks.append(refs[: 2 * places + 2])
        refs = refs[2 * places + 2 :]
    out_ref, done, sems = refs[1:]
    half = done.shape[1]
    copies = []
    for k, places in enumerate(sets):
        own_ref, *last_refs, c2_ref = blocks[k]
        for j in range(places):
            cols = slice(j * width, (j + 1) * width)
            n = len(copies)

            def put(row, ref):
                total = own_ref[row, :, cols].astype(jnp.float32) + ref[...].astype(jnp.float32)
                done[n + row] = total.astype(done.dtype)

            put(0, last_refs[j])
            for code, ref in enumerate((c2_ref.at[:, cols], last_refs[places + j])):

                @pl.when(pick[4] == code)
                def _():
                    put(1, ref)

            for row in range(2):
                to = place(pick, 2 * row, pick[5 + n // 2], out_ref, half, width)
                copies.append(pltpu.make_async_copy(done.at[n + row], to, sems.at[n + row]))
                copies[-1].start()
    for copy in copies:
        copy.wait()


def late_blocks(pick, out, owns, arrived, width):
    half = arrived[0][0].shape[0]
    sets = [len(blocks) // 2 for blocks in arrived]
    flat = [block for own, blocks in zip(owns, arrived) for block in (own, *blocks)]
    count = 2 * sum(sets)
    return pl.pallas_call(
        functools.partial(late_kernel, sets, width),
        in_specs=[SCALARS] + [HELD] * len(flat) + [ANYWHERE],
        out_specs=ANYWHERE,
        out_shape=jax.ShapeDtypeStruct(out.shape, out.dtype),
        input_output_aliases={1 + len(flat): 0},
        scratch_shapes=[pltpu.VMEM((count, half, width), out.dtype), pltpu.SemaphoreType.DMA((count,))],
        compiler_params=pltpu.CompilerParams(vmem_limit_bytes=LIMIT),
        cost_estimate=cost(2),
    )(pick, *near_core(*flat), out)


def shards(acts, kv_grads, layer_section, token_counts):
    sections = lax.axis_size("section")
    chips = lax.axis_size("tp") // 2
    pipe = lax.axis_index("pipe")
    section = lax.axis_index("section")
    z, core = lax.axis_index("tp") // 2, lax.axis_index("tp") % 2
    acts, kv = acts[0], kv_grads[0]
    width = kv.shape[2]
    counts = jnp.sum((layer_section == section).astype(jnp.int32), axis=1)
    own_count = lax.dynamic_index_in_dim(counts, pipe, 0, keepdims=False)
    other_count = lax.dynamic_index_in_dim(counts, 1 - pipe, 0, keepdims=False)
    heavy = own_count == 2
    matched = own_count == other_count
    limit = lax.dynamic_index_in_dim(token_counts, pipe, 0, keepdims=False)
    h = heavy.astype(jnp.int32)
    f_slot = jnp.where(heavy, section % 2, 0)
    m_slot = 1 - f_slot

    def across(array, name):
        pairs = [
            (p * sections + s, (1 - p) * sections + (s ^ 1)) for p in range(2) for s in range(sections)
        ]
        with jax.named_scope(name):
            return lax.ppermute(array, ("pipe", "section"), pairs)

    def beside(array, name):
        with jax.named_scope(name):
            return lax.ppermute(array, "section", [(s, s ^ 1) for s in range(sections)])

    def swapped(array, name):
        with jax.named_scope(name):
            return lax.ppermute(array, "tp", [(t, t ^ 1) for t in range(2 * chips)])

    def around(array, by, name):
        pairs = [(2 * i + c, (i + (by if c == 0 else -by)) % chips * 2 + c) for i in range(chips) for c in range(2)]
        with jax.named_scope(name):
            return lax.ppermute(array, "tp", pairs)

    def codes_of(relay):
        inside = z // 2 == 1 - relay
        even, same = z % 2 == 0, z % 2 == core
        pick = jnp.where
        codes = (
            pick(inside, 0, pick(same, 1, 2)),
            pick(inside, 0, 1),
            pick(inside, pick(same, 1, 0), 2),
            pick(inside == same, 0, 1),
        )
        up, down, far = (z + 1) % chips, (z + chips - 1) % chips, (z + 2) % chips
        sources = (
            pick(inside, z * 2 + core, pick(even, down * 2, up * 2 + 1)),
            pick(inside, z * 2 + 1 - core, far * 2 + core),
            pick(inside, pick(even, up * 2 + 1, down * 2), far * 2 + 1 - core),
            pick(inside == even, up * 2, down * 2 + 1),
        )
        return codes, sources

    slot_of = lambda role: jnp.where(role == 1, m_slot, f_slot)
    sent_codes, _ = codes_of(pipe)
    kept_codes, kept_sources = codes_of(1 - pipe)
    places = [source - pipe * chips for source in kept_sources]
    parts = ((0,), (1, 2), (3,))
    at_c1, at_c2, at_i2 = range(3)
    pick = functools.partial(jnp.where, heavy)
    roles = (pick(1, 0), 0, 1, pick(0, 1))
    halves = (0, pick(0, 1), pick(1, 0), 1)
    slots = tuple(slot_of(role) for role in roles)
    early = (jnp.where(matched, at_i2, at_c1), jnp.where(matched, at_c2, at_i2))
    early_to = (m_slot, 0, pick(f_slot, m_slot), pick(0, 1))
    late_to = (f_slot, 1, pick(m_slot, f_slot), h)
    sent, kept = [], []
    for part in parts:
        codes = [sent_codes[j] for j in part]
        sent += [scalars(*slots[:2], *codes), scalars(*slots[2:], *codes)]
        codes, spots = [kept_codes[j] for j in part], [places[j] for j in part]
        kept.append(scalars(*early_to, h, *slots, *codes, *early, *spots))
    last = [scalars(*late_to, matched, *places[:3]), scalars(*late_to, matched, *places[3:])]
    flag, turns, *sent = tied(scalars(1 - h), scalars(*slots, *halves, limit), *sent, *kept, *last)
    sent, kept, last = sent[: 2 * len(parts)], sent[2 * len(parts) : -2], sent[-2:]

    with jax.named_scope("turned"):
        turned = turn(turns, acts)

    def first_step(k, groups):
        with jax.named_scope(f"first_{k}"):
            c1, i1 = send_blocks(sent[2 * k], turned[:2], groups)
        pick2, c1, i1 = tied(sent[2 * k + 1], c1, i1)
        with jax.named_scope(f"second_{k}"):
            x2, s2 = send_blocks(pick2, turned[2:], groups)
        return across(c1, f"rc1_{k}"), beside(i1, f"ri1_{k}"), x2, s2

    def second_step(rc1, ri1, x2, s2):
        with jax.named_scope("chosen2"):
            return choose(flag, (x2, ri1), (s2, rc1))

    def third_step(rc1, ri1, rc2, ri2):
        with jax.named_scope("chosen3"):
            return choose(flag, (ri1, ri2), (rc1, rc2))

    def keep(k, groups, arrived, before):
        with jax.named_scope(f"kept_{k}"):
            return own_blocks(kept[k], turned, groups, arrived, chips * width, before)

    def finish(pick, out, owns, arrived):
        with jax.named_scope("joined"):
            return late_blocks(pick, out, owns, arrived, width)

    near, pair, *turned = tied(around(kv, 1, "near"), swapped(kv, "pair"), *turned)
    far = around(near, 1, "far")
    near_pair = swapped(near, "near_pair")
    set0 = [[kv, near, near_pair]]
    rc1_0, ri1_0, x2_0, s2_0 = first_step(0, set0)
    c2_0, i2_0 = second_step(rc1_0, ri1_0, x2_0, s2_0)
    rc2_0 = across(c2_0, "rc2_0")
    ri2_0 = beside(i2_0, "ri2_0")
    c3_0, i3_0 = third_step(rc1_0, ri1_0, rc2_0, ri2_0)
    rc3_0 = across(c3_0, "rc3_0")
    ri3_0 = beside(i3_0, "ri3_0")
    far = after(far, c3_0, i3_0)
    late = around(after(kv, far), -1, "late")
    far_pair = swapped(far, "far_pair")
    set1 = [[pair, far], [near, near_pair, far_pair]]
    rc1_1, ri1_1, x2_1, s2_1 = first_step(1, set1)
    out, own_0 = keep(0, set0, (rc1_0, rc2_0, ri2_0), None)
    rc3_0, ri3_0, own_0, rc1_1, ri1_1 = tied(rc3_0, ri3_0, own_0, rc1_1, ri1_1)
    c2_1, i2_1 = second_step(rc1_1, ri1_1, x2_1, s2_1)
    late = after(late, c2_1, i2_1)
    late_pair = swapped(late, "late_pair")
    set2 = [[late, late_pair]]
    rc1_2, ri1_2, x2_2, s2_2 = first_step(2, set2)
    rc2_1 = across(c2_1, "rc2_1")
    ri2_1 = beside(i2_1, "ri2_1")
    rc2_1, ri2_1, x2_2, s2_2 = tied(rc2_1, ri2_1, x2_2, s2_2)
    c3_1, c3_1b, i3_1, i3_1b = choose(flag, (ri1_1, ri2_1), (rc1_1, rc2_1), 2)
    rc3_1 = across(c3_1, "rc3_1")
    ri3_1 = beside(i3_1, "ri3_1")
    c2_2, i2_2 = second_step(rc1_2, ri1_2, x2_2, s2_2)
    rc2_2 = across(c2_2, "rc2_2")
    ri2_2 = beside(i2_2, "ri2_2")
    rc3_1, ri3_1, c3_1b, i3_1b = tied(rc3_1, ri3_1, c3_1b, i3_1b)
    rc3_1b = across(c3_1b, "rc3_1b")
    ri3_1b = beside(i3_1b, "ri3_1b")
    out, own_1 = keep(1, set1, (rc1_1, rc2_1, ri2_1), out)
    c3_2, i3_2 = third_step(rc1_2, ri1_2, rc2_2, ri2_2)
    rc3_2 = across(c3_2, "rc3_2")
    ri3_2 = beside(i3_2, "ri3_2")
    out, own_2 = keep(2, set2, (rc1_2, rc2_2, ri2_2), out)
    out = finish(last[0], out, (own_0, own_1), ((rc3_0, ri3_0, rc2_0), (rc3_1, rc3_1b, ri3_1, ri3_1b, rc2_1)))
    return finish(last[1], out, (own_2,), ((rc3_2, ri3_2, rc2_2),))


def solution(mesh):
    placed = (P("pipe", "section", None, "tp"), P("pipe", "section", None, "tp"), P(), P())
    return jax.shard_map(
        shards, mesh=mesh, in_specs=placed, out_specs=P("section", "tp", "pipe"), check_vma=False
    )
```

```python
import functools

import jax
import jax.numpy as jnp
from jax import lax
from jax.experimental import pallas as pl
from jax.experimental.pallas import tpu as pltpu
from jax.sharding import PartitionSpec as P

MIB = 1 << 20
LIMIT = 8 * MIB


def cost(micros):
    return pl.CostEstimate(flops=int(micros * 1.15e9), bytes_accessed=1, transcendentals=0)


def near_core(*arrays):
    return [pltpu.with_memory_space_constraint(array, pltpu.VMEM) for array in arrays]


SCALARS = pl.BlockSpec(memory_space=pltpu.SMEM)
HELD = pl.BlockSpec(memory_space=pltpu.VMEM)
ANYWHERE = pl.BlockSpec(memory_space=pl.ANY)


def tied(*values):
    return lax.optimization_barrier(values)


def after(value, *others):
    return tied(value, *others)[0]


def after_each(values, *others):
    return tied(*values, *others)[: len(values)]


def scalars(*values):
    return jnp.stack([jnp.asarray(v, jnp.int32) for v in values])


def turn_kernel(pick, *refs):
    refs, outs = refs[: len(refs) // 2], refs[len(refs) // 2 :]
    tile = refs[0].shape[1]
    rows = pl.program_id(0) * tile + lax.broadcasted_iota(jnp.int32, (tile, 1), 0)
    for x_ref, o_ref in zip(refs, outs):
        x = jnp.where(rows < pick[8], x_ref[0].astype(jnp.float32), 0.0)
        o_ref[...] = x.T.astype(o_ref.dtype)


def turn(pick, acts):
    _, tokens, feats = acts.shape
    tile, half = 256, feats // 2
    ins = [pl.BlockSpec((1, tile, half), functools.partial(lambda b, i, p: (p[b], i, p[4 + b]), b)) for b in range(4)]
    return pl.pallas_call(
        turn_kernel,
        grid_spec=pltpu.PrefetchScalarGridSpec(
            num_scalar_prefetch=1,
            grid=(tokens // tile,),
            in_specs=ins,
            out_specs=[pl.BlockSpec((half, tile), lambda i, p: (0, i))] * 4,
        ),
        out_shape=[pltpu.VMEM((half, tokens), acts.dtype)] * 4,
        compiler_params=pltpu.CompilerParams(vmem_limit_bytes=LIMIT),
        cost_estimate=cost(5),
    )(pick, *[acts] * 4)


def split(refs, counts):
    groups = []
    for count in counts:
        groups.append(refs[:count])
        refs = refs[count:]
    return groups, refs


def product(x_ref, kv_ref, slot):
    return jnp.dot(x_ref[...], kv_ref[slot], preferred_element_type=jnp.float32)


def send_kernel(counts, pick, *refs):
    xs, (groups, outs) = refs[:2], split(refs[2:], counts)
    width = groups[0][0].shape[2]
    for j, group in enumerate(groups):
        for code, kv_ref in enumerate(group):

            @pl.when(pick[2 + j] == code)
            def _():
                for step in range(2):
                    value = product(xs[step], kv_ref, pick[step])
                    outs[step][:, j * width : (j + 1) * width] = value.astype(outs[step].dtype)


def send_blocks(pick, xs, groups):
    half, _ = xs[0].shape
    width = groups[0][0].shape[2]
    flat = [array for group in groups for array in group]
    return pl.pallas_call(
        functools.partial(send_kernel, [len(group) for group in groups]),
        in_specs=[SCALARS] + [HELD] * (2 + len(flat)),
        out_specs=[HELD] * 2,
        out_shape=[pltpu.VMEM((half, len(groups) * width), xs[0].dtype)] * 2,
        compiler_params=pltpu.CompilerParams(vmem_limit_bytes=LIMIT),
        cost_estimate=cost(1.5 * len(groups)),
    )(pick, *near_core(*xs, *flat))


def choose_kernel(pieces, pick, *refs):
    width = refs[4].shape[1]
    for code in range(2):

        @pl.when(pick[0] == code)
        def _():
            for n, out_ref in enumerate(refs[4:]):
                at = n % pieces * width
                out_ref[...] = refs[2 * (n // pieces) + code][:, at : at + width]


def choose(flag, first, second, pieces=1):
    rows, cols = first[0].shape
    return pl.pallas_call(
        functools.partial(choose_kernel, pieces),
        in_specs=[SCALARS] + [HELD] * 4,
        out_specs=[HELD] * (2 * pieces),
        out_shape=[pltpu.VMEM((rows, cols // pieces), first[0].dtype)] * (2 * pieces),
        compiler_params=pltpu.CompilerParams(vmem_limit_bytes=LIMIT),
        cost_estimate=cost(0.5),
    )(flag, *near_core(*first, *second))


def place(pick, at, spot, out_ref, half, width):
    rows = pl.ds(pl.multiple_of(pick[at + 1] * half, half), half)
    cols = pl.ds(pl.multiple_of(spot * width, width), width)
    return out_ref.at[pick[at], rows, cols]


def own_kernel(counts, aliased, pick, *refs):
    xs, (groups, refs) = refs[:4], split(refs[4:], counts)
    arrived, (out_ref, late_ref, done, sems) = refs[:3], refs[3 + aliased :]
    half, width = done.shape[1:]
    heavy = pick[4] == 1
    base = 9
    for j, group in enumerate(groups):
        cols = slice(j * width, (j + 1) * width)
        for code, kv_ref in enumerate(group):
            here = pick[base + j] == code

            @pl.when(here & heavy)
            def _():
                for i in range(2):
                    value = product(xs[i], kv_ref, pick[5 + i]).astype(done.dtype)
                    done[2 * j + i] = value
                for i in range(2):
                    late_ref[i, :, cols] = product(xs[3 - i], kv_ref, pick[8 - i]).astype(done.dtype)

            @pl.when(here & jnp.logical_not(heavy))
            def _():
                for i in range(2):
                    late_ref[i, :, cols] = product(xs[1 - i], kv_ref, pick[6 - i]).astype(done.dtype)

        @pl.when(jnp.logical_not(heavy))
        def _():
            for i in range(2):
                done[2 * j + i] = jnp.zeros(done.shape[1:], done.dtype)

        for i in range(2):
            for choice, ref in enumerate(arrived):

                @pl.when(heavy & (pick[base + len(counts) + i] == choice))
                def _():
                    total = done[2 * j + i].astype(jnp.float32) + ref[:, cols].astype(jnp.float32)
                    done[2 * j + i] = total.astype(done.dtype)

            spot = pick[base + len(counts) + 2 + j]
            pltpu.make_async_copy(done.at[2 * j + i], place(pick, 2 * i, spot, out_ref, half, width), sems.at[2 * j + i]).start()

    for j in range(len(groups)):
        for i in range(2):
            spot = pick[base + len(counts) + 2 + j]
            pltpu.make_async_copy(done.at[2 * j + i], place(pick, 2 * i, spot, out_ref, half, width), sems.at[2 * j + i]).wait()


def own_blocks(pick, xs, groups, arrived, out_cols, before):
    half, _ = xs[0].shape
    dtype = xs[0].dtype
    width = groups[0][0].shape[2]
    counts = [len(group) for group in groups]
    flat = [array for group in groups for array in group]
    held = [] if before is None else [before]
    return pl.pallas_call(
        functools.partial(own_kernel, counts, len(held)),
        in_specs=[SCALARS] + [HELD] * (4 + len(flat) + len(arrived)) + [ANYWHERE] * len(held),
        out_specs=[ANYWHERE, HELD],
        out_shape=[
            jax.ShapeDtypeStruct((2, 2 * half, out_cols), dtype),
            pltpu.VMEM((2, half, len(groups) * width), dtype),
        ],
        input_output_aliases={5 + len(flat) + len(arrived): 0} if held else {},
        scratch_shapes=[
            pltpu.VMEM((2 * len(groups), half, width), dtype),
            pltpu.SemaphoreType.DMA((2 * len(groups),)),
        ],
        compiler_params=pltpu.CompilerParams(vmem_limit_bytes=LIMIT),
        cost_estimate=cost(2.5 * len(groups)),
    )(pick, *near_core(*xs, *flat, *arrived), *held)


def late_kernel(sets, width, pick, *refs):
    blocks = []
    for places in sets:
        blocks.append(refs[: 2 * places + 2])
        refs = refs[2 * places + 2 :]
    out_ref, done, sems = refs[1:]
    half = done.shape[1]
    copies = []
    for k, places in enumerate(sets):
        own_ref, *last_refs, c2_ref = blocks[k]
        for j in range(places):
            cols = slice(j * width, (j + 1) * width)
            n = len(copies)

            def put(row, ref):
                total = own_ref[row, :, cols].astype(jnp.float32) + ref[...].astype(jnp.float32)
                done[n + row] = total.astype(done.dtype)

            put(0, last_refs[j])
            for code, ref in enumerate((c2_ref.at[:, cols], last_refs[places + j])):

                @pl.when(pick[4] == code)
                def _():
                    put(1, ref)

            for row in range(2):
                to = place(pick, 2 * row, pick[5 + n // 2], out_ref, half, width)
                copies.append(pltpu.make_async_copy(done.at[n + row], to, sems.at[n + row]))
                copies[-1].start()
    for copy in copies:
        copy.wait()


def late_blocks(pick, out, owns, arrived, width):
    half = arrived[0][0].shape[0]
    sets = [len(blocks) // 2 for blocks in arrived]
    flat = [block for own, blocks in zip(owns, arrived) for block in (own, *blocks)]
    count = 2 * sum(sets)
    return pl.pallas_call(
        functools.partial(late_kernel, sets, width),
        in_specs=[SCALARS] + [HELD] * len(flat) + [ANYWHERE],
        out_specs=ANYWHERE,
        out_shape=jax.ShapeDtypeStruct(out.shape, out.dtype),
        input_output_aliases={1 + len(flat): 0},
        scratch_shapes=[pltpu.VMEM((count, half, width), out.dtype), pltpu.SemaphoreType.DMA((count,))],
        compiler_params=pltpu.CompilerParams(vmem_limit_bytes=LIMIT),
        cost_estimate=cost(2),
    )(pick, *near_core(*flat), out)


def shards(acts, kv_grads, layer_section, token_counts):
    sections = lax.axis_size("section")
    chips = lax.axis_size("tp") // 2
    pipe = lax.axis_index("pipe")
    section = lax.axis_index("section")
    z, core = lax.axis_index("tp") // 2, lax.axis_index("tp") % 2
    acts, kv = acts[0], kv_grads[0]
    width = kv.shape[2]
    counts = jnp.sum((layer_section == section).astype(jnp.int32), axis=1)
    own_count = lax.dynamic_index_in_dim(counts, pipe, 0, keepdims=False)
    other_count = lax.dynamic_index_in_dim(counts, 1 - pipe, 0, keepdims=False)
    heavy = own_count == 2
    matched = own_count == other_count
    limit = lax.dynamic_index_in_dim(token_counts, pipe, 0, keepdims=False)
    h = heavy.astype(jnp.int32)
    f_slot = jnp.where(heavy, section % 2, 0)
    m_slot = 1 - f_slot

    def across(array, name):
        pairs = [
            (p * sections + s, (1 - p) * sections + (s ^ 1)) for p in range(2) for s in range(sections)
        ]
        with jax.named_scope(name):
            return lax.ppermute(array, ("pipe", "section"), pairs)

    def beside(array, name):
        with jax.named_scope(name):
            return lax.ppermute(array, "section", [(s, s ^ 1) for s in range(sections)])

    def swapped(array, name):
        with jax.named_scope(name):
            return lax.ppermute(array, "tp", [(t, t ^ 1) for t in range(2 * chips)])

    def around(array, by, name):
        pairs = [(2 * i + c, (i + (by if c == 0 else -by)) % chips * 2 + c) for i in range(chips) for c in range(2)]
        with jax.named_scope(name):
            return lax.ppermute(array, "tp", pairs)

    def codes_of(relay):
        inside = z // 2 == 1 - relay
        even, same = z % 2 == 0, z % 2 == core
        pick = jnp.where
        codes = (
            pick(inside, 0, pick(same, 1, 2)),
            pick(inside, 0, 1),
            pick(inside, pick(same, 1, 0), 2),
            pick(inside == same, 0, 1),
        )
        up, down, far = (z + 1) % chips, (z + chips - 1) % chips, (z + 2) % chips
        sources = (
            pick(inside, z * 2 + core, pick(even, down * 2, up * 2 + 1)),
            pick(inside, z * 2 + 1 - core, far * 2 + core),
            pick(inside, pick(even, up * 2 + 1, down * 2), far * 2 + 1 - core),
            pick(inside == even, up * 2, down * 2 + 1),
        )
        return codes, sources

    slot_of = lambda role: jnp.where(role == 1, m_slot, f_slot)
    sent_codes, _ = codes_of(pipe)
    kept_codes, kept_sources = codes_of(1 - pipe)
    places = [source - pipe * chips for source in kept_sources]
    parts = ((0,), (1, 2), (3,))
    at_c1, at_c2, at_i2 = range(3)
    pick = functools.partial(jnp.where, heavy)
    roles = (pick(1, 0), 0, 1, pick(0, 1))
    halves = (0, pick(0, 1), pick(1, 0), 1)
    slots = tuple(slot_of(role) for role in roles)
    early = (jnp.where(matched, at_i2, at_c1), jnp.where(matched, at_c2, at_i2))
    early_to = (m_slot, 0, pick(f_slot, m_slot), pick(0, 1))
    late_to = (f_slot, 1, pick(m_slot, f_slot), h)
    sent, kept = [], []
    for part in parts:
        codes = [sent_codes[j] for j in part]
        sent += [scalars(*slots[:2], *codes), scalars(*slots[2:], *codes)]
        codes, spots = [kept_codes[j] for j in part], [places[j] for j in part]
        kept.append(scalars(*early_to, h, *slots, *codes, *early, *spots))
    last = [scalars(*late_to, matched, *places[:3]), scalars(*late_to, matched, *places[3:])]
    flag, turns, *sent = tied(scalars(1 - h), scalars(*slots, *halves, limit), *sent, *kept, *last)
    sent, kept, last = sent[: 2 * len(parts)], sent[2 * len(parts) : -2], sent[-2:]

    with jax.named_scope("turned"):
        turned = turn(turns, acts)

    def first_step(k, groups):
        with jax.named_scope(f"first_{k}"):
            c1, i1 = send_blocks(sent[2 * k], turned[:2], groups)
        pick2, c1, i1 = tied(sent[2 * k + 1], c1, i1)
        with jax.named_scope(f"second_{k}"):
            x2, s2 = send_blocks(pick2, turned[2:], groups)
        return across(c1, f"rc1_{k}"), beside(i1, f"ri1_{k}"), x2, s2

    def second_step(rc1, ri1, x2, s2):
        with jax.named_scope("chosen2"):
            return choose(flag, (x2, ri1), (s2, rc1))

    def third_step(rc1, ri1, rc2, ri2):
        with jax.named_scope("chosen3"):
            return choose(flag, (ri1, ri2), (rc1, rc2))

    def keep(k, groups, arrived, before):
        with jax.named_scope(f"kept_{k}"):
            return own_blocks(kept[k], turned, groups, arrived, chips * width, before)

    def finish(pick, out, owns, arrived):
        with jax.named_scope("joined"):
            return late_blocks(pick, out, owns, arrived, width)

    near, *turned = tied(around(kv, 1, "near"), *turned)
    far = around(near, 1, "far")
    near_pair = swapped(near, "near_pair")
    set0 = [[kv, near, near_pair]]
    rc1_0, ri1_0, x2_0, s2_0 = first_step(0, set0)
    c2_0, i2_0 = second_step(rc1_0, ri1_0, x2_0, s2_0)
    rc2_0 = across(c2_0, "rc2_0")
    ri2_0 = beside(i2_0, "ri2_0")
    c3_0, i3_0 = third_step(rc1_0, ri1_0, rc2_0, ri2_0)
    rc3_0 = across(c3_0, "rc3_0")
    ri3_0 = beside(i3_0, "ri3_0")
    far = after(far, c3_0, i3_0)
    late = around(after(kv, far), -1, "late")
    pair, far = tied(swapped(after(kv, near_pair), "pair"), far)
    far_pair = swapped(far, "far_pair")
    set1 = [[pair, far], [near, near_pair, far_pair]]
    rc1_1, ri1_1, x2_1, s2_1 = first_step(1, set1)
    out, own_0 = keep(0, set0, (rc1_0, rc2_0, ri2_0), None)
    rc3_0, ri3_0, own_0, rc1_1, ri1_1 = tied(rc3_0, ri3_0, own_0, rc1_1, ri1_1)
    c2_1, i2_1 = second_step(rc1_1, ri1_1, x2_1, s2_1)
    late = after(late, c2_1, i2_1)
    late_pair = swapped(late, "late_pair")
    set2 = [[late, late_pair]]
    rc1_2, ri1_2, x2_2, s2_2 = first_step(2, set2)
    rc2_1 = across(c2_1, "rc2_1")
    ri2_1 = beside(i2_1, "ri2_1")
    rc2_1, ri2_1, x2_2, s2_2 = tied(rc2_1, ri2_1, x2_2, s2_2)
    c3_1, c3_1b, i3_1, i3_1b = choose(flag, (ri1_1, ri2_1), (rc1_1, rc2_1), 2)
    rc3_1 = across(c3_1, "rc3_1")
    ri3_1 = beside(i3_1, "ri3_1")
    c2_2, i2_2 = second_step(rc1_2, ri1_2, x2_2, s2_2)
    rc2_2 = across(c2_2, "rc2_2")
    ri2_2 = beside(i2_2, "ri2_2")
    rc3_1, ri3_1, c3_1b, i3_1b = tied(rc3_1, ri3_1, c3_1b, i3_1b)
    rc3_1b = across(c3_1b, "rc3_1b")
    ri3_1b = beside(i3_1b, "ri3_1b")
    out, own_1 = keep(1, set1, (rc1_1, rc2_1, ri2_1), out)
    c3_2, i3_2 = third_step(rc1_2, ri1_2, rc2_2, ri2_2)
    rc3_2 = across(c3_2, "rc3_2")
    ri3_2 = beside(i3_2, "ri3_2")
    out, own_2 = keep(2, set2, (rc1_2, rc2_2, ri2_2), out)
    out = finish(last[0], out, (own_0, own_1), ((rc3_0, ri3_0, rc2_0), (rc3_1, rc3_1b, ri3_1, ri3_1b, rc2_1)))
    return finish(last[1], out, (own_2,), ((rc3_2, ri3_2, rc2_2),))


def solution(mesh):
    placed = (P("pipe", "section", None, "tp"), P("pipe", "section", None, "tp"), P(), P())
    return jax.shard_map(
        shards, mesh=mesh, in_specs=placed, out_specs=P("section", "tp", "pipe"), check_vma=False
    )
```
